256 devices in a mesh: member: 64 (over y, z, core), slab: 4 (over x).
Axes of the slice: x: 4, y: 4, z: 8, core: 2. Of those that a mesh axis runs over, the one named last changes fastest.
Arguments:
- ensemble_obs: bfloat16 [512, 4, 32768], P('member', 'slab'), may hold values from -6 to 6
- obs_values: bfloat16 [2, 4, 32768], P(None, 'slab', 'member'), may hold values from -9 to 9
- obs_index: int32 [4, 128, 512], P('slab', 'member'), may hold values from 0 to 1023, as said below
- obs_count: int32 [4, 128], P('slab', 'member'), may hold values from 1 to 512, as said below
- loc_weight: float32 [4, 128, 512], P('slab', 'member'), may hold values from 0.05 to 1
- state: bfloat16 [512, 4, 128, 2048], P('member', 'slab'), may hold values from -6 to 6
Outputs:
- analysis: bfloat16 [512, 4, 128, 2048], P('member', 'slab')
The draws below stay inside these ranges and needn't reach their ends.
Inputs may be any that keep to these rules, and one draw needn't show every extreme that they name: `obs_index`: each block's first slot holds position 0 for even block numbers and 1023 for odd ones. `obs_count`: every strip has a block that uses all 512 slots.
All inputs are finite; a program needn't handle non-finite values.
Results may differ from the reference program's by a relative error of at most 0.019.
Values may be sent and summed in bfloat16 or wider, within the bound.
A program may use at most 64 MiB of HBM per device.

```python
import math
import jax
import jax.numpy as jnp
from jax import lax

K = 512
BLK_DEV = 2
CELLS = 2048
OBS_DEV = 512
ITERS = 3
RIM = 256
POOL = 1024
PMAX = 512
BLOCKS = 128
OBS_STRIP = 32768
N_MEMBER = 64
N_SLAB = 4


def draw_obs_values(key, part):
    key = jax.random.fold_in(key, 11)
    first, second = jax.random.split(key)
    shape = (N_SLAB, N_MEMBER * OBS_DEV)
    observed = 3.0 * jnp.clip(jax.random.normal(first, shape, jnp.float32), -3.0, 3.0)
    inverse = jnp.exp(jax.random.uniform(second, shape, jnp.float32, math.log(0.25), math.log(4.0)))
    return jnp.stack([observed, inverse]).astype(jnp.bfloat16)


def draw_obs_index(key, part):
    key = jax.random.fold_in(key, 13)
    raw = jax.random.randint(key, (N_SLAB, N_MEMBER * BLK_DEV, PMAX), 0, POOL, dtype=jnp.int32)
    blocks = jnp.arange(N_MEMBER * BLK_DEV, dtype=jnp.int32)
    edge = jnp.where(blocks % 2 == 0, 0, POOL - 1).astype(jnp.int32)
    first_slot = jnp.broadcast_to(edge[None, :], (N_SLAB, N_MEMBER * BLK_DEV))
    return raw.at[:, :, 0].set(first_slot)


def draw_obs_count(key, part):
    key = jax.random.fold_in(key, 17)
    first, second = jax.random.split(key)
    counts = jax.random.randint(first, (N_SLAB, N_MEMBER * BLK_DEV), 1, PMAX + 1, dtype=jnp.int32)
    fullest = jax.random.randint(second, (N_SLAB, 1), 0, N_MEMBER * BLK_DEV, dtype=jnp.int32)
    blocks = jnp.arange(N_MEMBER * BLK_DEV, dtype=jnp.int32)[None, :]
    return jnp.where(blocks == fullest, PMAX, counts).astype(jnp.int32)


def block_scale(own_key, extent, cuts, low, high):
    factor_of, own = 1.0, jax.random.fold_in(own_key, 6)
    for position, shards_of in cuts:
        steps = jnp.exp(jax.random.uniform(jax.random.fold_in(own, position), (shards_of,), jnp.float32, low / len(cuts), high / len(cuts)))
        factor_of = factor_of * jnp.repeat(steps, extent[position] // shards_of).reshape([-1 if axis == position else 1 for axis in range(len(extent))])
    return factor_of


def centred(key, shape, scale, reach, shards=(), kind=jnp.bfloat16):
    values = scale * jax.random.normal(key, shape, jnp.float32)
    if shards:
        values = values * block_scale(key, shape, shards, -0.22, 0.18)
    return jnp.clip(values, -reach, reach).astype(kind)


def setup_inputs(seed: int = 0) -> dict:
    seeds = jax.random.split(jax.random.key(seed), 7)
    ensemble_obs = centred(seeds[0], (K, N_SLAB, OBS_STRIP), 1.0, 6.0, ((0, 64), (1, 4)))
    obs_values = draw_obs_values(jax.random.fold_in(seeds[6], 71), 0)
    obs_index = draw_obs_index(jax.random.fold_in(seeds[6], 71), 0)
    obs_count = draw_obs_count(jax.random.fold_in(seeds[6], 71), 0)
    loc_weight = jnp.clip(jnp.exp(math.log(1.0) - 2.9957323 * jax.random.uniform(seeds[4], (N_SLAB, BLOCKS, PMAX), jnp.float32) ** block_scale(seeds[4], (N_SLAB, BLOCKS, PMAX), ((0, 4), (1, 64)), -0.2, 0.2)), 0.05, 1.0)
    state = centred(seeds[5], (K, N_SLAB, BLOCKS, CELLS), 1.0, 6.0, ((0, 64), (1, 4)))
    return {"ensemble_obs": ensemble_obs, "obs_values": obs_values, "obs_index": obs_index, "obs_count": obs_count, "loc_weight": loc_weight, "state": state}


def block_transform(pool, index, count, local):
    members = pool.shape[0] - 2
    chosen = jnp.take(pool, index, axis=1)
    hmean = lax.optimization_barrier(jnp.sum(chosen[:members].astype(jnp.float32), axis=0)) / members
    pert = (chosen[:members].astype(jnp.float32) - hmean).astype(jnp.bfloat16)
    depart = chosen[members].astype(jnp.float32) - hmean
    slots = jnp.arange(index.shape[0], dtype=jnp.int32)
    weight = jnp.where(slots < count, local * chosen[members + 1].astype(jnp.float32), jnp.float32(0.0))
    weighted = (pert.astype(jnp.float32) * weight).astype(jnp.bfloat16)
    identity = jnp.eye(members, dtype=jnp.float32)
    gram = jnp.dot(pert, weighted.T, preferred_element_type=jnp.float32) + (members - 1.0) * identity
    drive = jnp.dot(weighted.astype(jnp.float32), depart, precision=lax.Precision.HIGHEST)
    scale = jnp.sqrt(jnp.sum(gram * gram))
    matrix = gram / scale
    inverse = identity
    for step in range(ITERS):
        factor = 1.5 * identity - 0.5 * jnp.dot(inverse, matrix, precision=lax.Precision.HIGHEST)
        matrix = jnp.dot(matrix, factor, precision=lax.Precision.HIGHEST)
        inverse = jnp.dot(factor, inverse, precision=lax.Precision.HIGHEST)
    spread = jnp.sqrt((members - 1.0) / scale) * inverse
    inner = jnp.dot(inverse, drive, precision=lax.Precision.HIGHEST)
    shift = jnp.dot(inverse, inner, precision=lax.Precision.HIGHEST) / scale
    return (spread + shift[:, None]).astype(jnp.bfloat16)

def apply_block(pair):
    weights, columns = pair
    members = columns.shape[0]
    smean = lax.optimization_barrier(jnp.sum(columns.astype(jnp.float32), axis=0)) / members
    spert = (columns.astype(jnp.float32) - smean).astype(jnp.bfloat16)
    result = smean + jnp.dot(weights.T, spert, preferred_element_type=jnp.float32)
    return result.astype(jnp.bfloat16)

def reference(ensemble_obs, obs_values, obs_index, obs_count, loc_weight, state):
    members = ensemble_obs.shape[0]
    stacked = jnp.concatenate([ensemble_obs, obs_values], axis=0)
    regions = stacked.reshape(members + 2, N_SLAB, N_MEMBER, OBS_DEV)
    left = jnp.roll(regions[..., OBS_DEV - RIM:], 1, axis=1)
    right = jnp.roll(regions[..., :RIM], -1, axis=1)
    pools = jnp.concatenate([left, regions, right], axis=3)
    pools = jnp.transpose(pools, (1, 2, 0, 3)).reshape(N_SLAB * N_MEMBER, members + 2, POOL)
    index = obs_index.reshape(N_SLAB * N_MEMBER, BLK_DEV, PMAX)
    count = obs_count.reshape(N_SLAB * N_MEMBER, BLK_DEV)
    local = loc_weight.reshape(N_SLAB * N_MEMBER, BLK_DEV, PMAX)

    def region_transforms(item):
        pool, idx, cnt, loc = item
        return jax.vmap(block_transform, in_axes=(None, 0, 0, 0))(pool, idx, cnt, loc)
    weights = lax.map(region_transforms, (pools, index, count, local))
    weights = weights.reshape(N_SLAB * N_MEMBER * BLK_DEV, members, members)
    blocks = jnp.transpose(state, (1, 2, 0, 3)).reshape(N_SLAB * N_MEMBER * BLK_DEV, members, CELLS)
    updated = lax.map(apply_block, (weights, blocks))
    updated = updated.reshape(N_SLAB, N_MEMBER * BLK_DEV, members, CELLS)
    return jnp.transpose(updated, (2, 0, 1, 3))
```

```python
import functools

import jax
import jax.numpy as jnp
from jax import lax
from jax.experimental import pallas as pl
from jax.experimental.pallas import tpu as pltpu
from jax.sharding import PartitionSpec as P

MESH = pl.DeviceIdType.MESH
F32 = jnp.float32
BF16 = jnp.bfloat16
HIGHEST = lax.Precision.HIGHEST

PEERS = 64
SLABS = 4
ROWS = 8
K = 512
BLKS = 2
MSG = BLKS * ROWS
CELLS = 2048
PIECES = 4
W = CELLS // PIECES
RIM = 256
POOL = 1024
GROUP = 8
GROUPS = PEERS // GROUP


def nt(a, b, precision=None):
    return lax.dot_general(
        a, b, (((1,), (1,)), ((), ())), precision=precision, preferred_element_type=F32
    )


def mm(a, b):
    return jnp.dot(a, b, precision=HIGHEST, preferred_element_type=F32)


def iota(shape, axis):
    return lax.broadcasted_iota(jnp.int32, shape, axis)


def split3(row, width):
    full = jnp.broadcast_to(row, (16, width))
    high = full.astype(BF16).astype(F32)
    rest = full - high
    mid = rest.astype(BF16).astype(F32)
    low = rest - mid
    r = iota((16, width), 0)
    rows = jnp.where(r == 0, high, jnp.where(r == 1, mid, jnp.where(r == 2, low, 0.0)))
    return rows.astype(BF16)


def gather_rows(inverse):
    n = GROUP * MSG
    out, src = iota((n, n), 0), iota((n, n), 1)
    if inverse:
        out, src = src, out
    wanted = (out % ROWS) * MSG + out // ROWS
    return jnp.where(src == wanted, 1.0, 0.0).astype(BF16)


def exchange(
    state, obs, vals, idx, cnt, loc, back,
    stage, fsend, frecv, bsend, osend, orecv, hsend, hrecv,
    pert, wgt, mats, expand, tbigf, tbig, spert,
    st_sem, fs_sem, fr_sem, fl_sem, bs_sem, br_sem, bl_sem,
    os_sem, or_sem, ol_sem, hs_sem, hr_sem,
):
    me = lax.axis_index("member")
    slab = lax.axis_index("slab")
    right = lax.rem(slab + 1, SLABS)
    left = lax.rem(slab + SLABS - 1, SLABS)

    barrier = pltpu.get_barrier_semaphore()

    def greet(i, carry):
        pl.semaphore_signal(
            barrier, inc=1, device_id={"member": lax.rem(me + 27 * i, PEERS)}, device_id_type=MESH
        )
        return carry

    lax.fori_loop(1, PEERS, greet, 0)
    for neighbour in (left, right):
        pl.semaphore_signal(barrier, inc=1, device_id={"slab": neighbour}, device_id_type=MESH)

    def stage_copy(p):
        cols = pl.ds(p * W, W)
        return pltpu.make_async_copy(
            state.at[:, 0, :, cols], stage.at[:, :, cols], st_sem.at[p]
        )

    for p in range(PIECES):
        stage_copy(p).start()

    def fill_obs(r, carry):
        a = obs[:, pl.ds(pl.multiple_of(r * 2 * RIM, 2 * RIM), RIM)].astype(F32)
        b = obs[:, pl.ds(pl.multiple_of(r * 2 * RIM + RIM, RIM), RIM)].astype(F32)
        osend[r] = jnp.concatenate([a, b], axis=0).astype(BF16)
        return carry

    lax.fori_loop(0, PEERS, fill_obs, 0)
    pl.semaphore_wait(barrier, PEERS - 1 + 2)

    own_obs = pltpu.make_async_copy(osend.at[me], orecv.at[me], ol_sem)
    own_obs.start()

    def send_obs(i, carry):
        d = lax.rem(me + 27 * i, PEERS)
        pltpu.make_async_remote_copy(
            src_ref=osend.at[d], dst_ref=orecv.at[me], send_sem=os_sem, recv_sem=or_sem,
            device_id={"member": d}, device_id_type=MESH,
        ).start()
        return carry

    lax.fori_loop(1, PEERS, send_obs, 0)

    def forward(p):
        stage_copy(p).wait()
        cols = pl.ds(p * W, W)

        def group(i, carry):
            g = lax.rem(me // GROUP + i, GROUPS)
            first = pl.multiple_of(g * GROUP, GROUP)
            rows = stage[:, pl.ds(pl.multiple_of(g * MSG, MSG), MSG), cols]
            moved = jnp.dot(
                gather_rows(False), rows.reshape(GROUP * MSG, W), preferred_element_type=F32
            )
            fsend[p, pl.ds(first, GROUP)] = moved.astype(BF16).reshape(GROUP, MSG, W)

            def one(j, inner):
                d = first + j

                @pl.when(d != me)
                def _():
                    pltpu.make_async_remote_copy(
                        src_ref=fsend.at[p, d], dst_ref=frecv.at[p, me],
                        send_sem=fs_sem.at[p], recv_sem=fr_sem.at[p],
                        device_id={"member": d}, device_id_type=MESH,
                    ).start()

                return inner

            lax.fori_loop(0, GROUP, one, 0)
            return carry

        lax.fori_loop(0, GROUPS, group, 0)
        pltpu.make_async_copy(fsend.at[p, me], frecv.at[p, me], fl_sem.at[p]).start()

    forward(0)

    own_obs.wait()
    most = pl.ds(0, PEERS - 1)
    pltpu.make_async_copy(osend.at[most], orecv.at[most], or_sem).wait()

    def halves(i, carry):
        x = orecv[pl.ds(i * 8, 8)].astype(F32)
        rows = pl.ds(pl.multiple_of(i * 64, 64), 64)
        hsend[1, rows] = x[:, :ROWS].reshape(64, RIM).astype(BF16)
        hsend[0, rows] = x[:, ROWS:].reshape(64, RIM).astype(BF16)
        return carry

    lax.fori_loop(0, 8, halves, 0)
    v = vals[...].astype(F32)
    for side, at in ((1, 0), (0, RIM)):
        r = iota((16, RIM), 0)
        first, second = v[0:1, at : at + RIM], v[1:2, at : at + RIM]
        hsend[side, K : K + 16] = jnp.where(
            r == 0, first, jnp.where(r == 1, second, 0.0)
        ).astype(BF16)
    halos = [
        pltpu.make_async_remote_copy(
            src_ref=hsend.at[side], dst_ref=hrecv.at[side],
            send_sem=hs_sem.at[side], recv_sem=hr_sem.at[side],
            device_id={"slab": to}, device_id_type=MESH,
        )
        for side, to in ((0, right), (1, left))
    ]
    for halo in halos:
        halo.start()

    for p in range(1, PIECES):
        forward(p)

    def fill_expand(i, carry):
        j = iota((64, POOL), 0) + i * 64
        c = iota((64, POOL), 1)
        rows = pl.ds(pl.multiple_of(i * 64, 64), 64)
        for b in range(BLKS):
            at = (j // ROWS) * MSG + b * ROWS + j % ROWS
            expand[b, rows] = jnp.where(c == at, 1.0, 0.0).astype(BF16)
        return carry

    lax.fori_loop(0, K // 64, fill_expand, 0)

    for halo in halos:
        halo.wait()

    departs, inverses = [], []
    for q, ref in enumerate((hrecv.at[0], hsend.at[1], hsend.at[0], hrecv.at[1])):
        x = ref[:K].astype(F32)
        mean = jnp.sum(x, axis=0, keepdims=True) * (1.0 / K)
        pert[:, q * RIM : (q + 1) * RIM] = (x - mean).astype(BF16)
        tail = ref[K : K + 16].astype(F32)
        departs.append(tail[0:1] - mean)
        inverses.append(tail[1:2])
    depart = split3(jnp.concatenate(departs, axis=1), POOL)

    diagonal = iota((K, K), 0) == iota((K, K), 1)
    for b in range(BLKS):
        row = idx[b : b + 1, :]
        slot = iota((1, 512), 1)
        local = jnp.where(slot < cnt[0, b], loc[b : b + 1, :], 0.0)
        local = split3(local, 512)
        for q in range(4):
            hit = iota((RIM, 512), 0) + q * RIM == row
            hit = jnp.where(hit, 1.0, 0.0).astype(BF16)
            total = nt(local, hit)
            weight = inverses[q] * (total[0:1] + total[1:2] + total[2:3])
            cols = slice(q * RIM, (q + 1) * RIM)
            wgt[b, :, cols] = (pert[:, cols].astype(F32) * weight).astype(BF16)

    def transform(b, carry):
        weighted = wgt[b]
        drive = nt(depart, weighted)
        drive = jnp.broadcast_to(drive[0:1] + drive[1:2] + drive[2:3], (8, K))
        gram = nt(pert[...], weighted) + jnp.where(diagonal, K - 1.0, 0.0)
        scale = jnp.sum(gram * gram, axis=1, keepdims=True)
        scale = jnp.sqrt(jnp.sum(scale, axis=0, keepdims=True))
        matrix = gram * (1.0 / scale)
        factor = jnp.where(diagonal, 1.5, 0.0) - 0.5 * matrix
        mats[1] = factor
        mats[0] = mm(matrix, factor)
        mats[2] = jnp.where(diagonal, 1.5, 0.0) - 0.5 * mm(mats[1], mats[0])
        mats[0] = mm(mats[0], mats[2])
        mats[1] = mm(mats[2], mats[1])
        mats[2] = jnp.where(diagonal, 1.5, 0.0) - 0.5 * mm(mats[1], mats[0])
        mats[0] = mm(mats[2], mats[1])
        inverse = mats[0]
        inner = nt(drive, inverse, HIGHEST)
        shift = nt(inner, inverse, HIGHEST)[0:1] / scale
        spread = jnp.sqrt((K - 1.0) / scale)
        mats[1] = spread * inverse.T + shift

        def widen(i, inner_carry):
            rows = mats[1, pl.ds(pl.multiple_of(i * 128, 128), 128)].astype(BF16)
            wide = jnp.dot(rows, expand[b], preferred_element_type=F32)
            at = pl.ds(pl.multiple_of(b * ROWS, ROWS), ROWS)
            tbigf[pl.ds(i * 16, 16), at] = wide.reshape(16, ROWS, POOL)
            return inner_carry

        lax.fori_loop(0, 4, widen, 0)
        return carry

    lax.fori_loop(0, BLKS, transform, 0)

    def narrow(i, carry):
        rows = pl.ds(pl.multiple_of(i * 128, 128), 128)
        tbig[rows] = tbigf[pl.ds(i * 8, 8)].reshape(128, POOL).astype(BF16)
        return carry

    lax.fori_loop(0, 8, narrow, 0)

    for p in range(PIECES):
        pltpu.make_async_copy(fsend.at[p, me], frecv.at[p, me], fl_sem.at[p]).wait()
        pltpu.make_async_copy(fsend.at[p, most], frecv.at[p, most], fr_sem.at[p]).wait()

        def add_up(i, total):
            x = frecv[p, pl.ds(i * 4, 4)].astype(F32)
            return total + jnp.sum(x, axis=0)

        total = lax.fori_loop(0, 16, add_up, jnp.zeros((MSG, W), F32))
        means = [
            jnp.sum(total[b * ROWS : (b + 1) * ROWS], axis=0, keepdims=True) * (1.0 / K)
            for b in range(BLKS)
        ]
        mean = jnp.concatenate([jnp.broadcast_to(m, (ROWS, W)) for m in means], axis=0)

        def less_mean(i, carry):
            x = frecv[p, pl.ds(i * 4, 4)].astype(F32) - mean[None]
            spert[pl.ds(pl.multiple_of(i * 64, 64), 64)] = x.reshape(64, W).astype(BF16)
            return carry

        lax.fori_loop(0, 16, less_mean, 0)

        def apply(i, carry):
            part = lax.rem(me // 16 + i, 4)
            rows = tbig[pl.ds(pl.multiple_of(part * 256, 256), 256)]
            moved = jnp.dot(rows, spert[...], preferred_element_type=F32)
            new = moved.reshape(16, MSG, W) + mean[None]
            first = pl.multiple_of(part * 16, 16)
            bsend[p, pl.ds(first, 16)] = new.astype(BF16)

            def one(j, inner):
                d = first + lax.rem(j * 7 + me, 16)

                @pl.when(d != me)
                def _():
                    pltpu.make_async_remote_copy(
                        src_ref=bsend.at[p, d], dst_ref=back.at[p, me],
                        send_sem=bs_sem.at[p], recv_sem=br_sem.at[p],
                        device_id={"member": d}, device_id_type=MESH,
                    ).start()

                return inner

            lax.fori_loop(0, 16, one, 0)
            return carry

        lax.fori_loop(0, 4, apply, 0)
        pltpu.make_async_copy(bsend.at[p, me], back.at[p, me], bl_sem.at[p]).start()

    pltpu.make_async_copy(osend.at[most], orecv.at[most], os_sem).wait()
    for p in range(PIECES):
        pltpu.make_async_copy(fsend.at[p, most], frecv.at[p, most], fs_sem.at[p]).wait()
        pltpu.make_async_copy(bsend.at[p, most], back.at[p, most], bs_sem.at[p]).wait()
        pltpu.make_async_copy(bsend.at[p, me], back.at[p, me], bl_sem.at[p]).wait()
        pltpu.make_async_copy(bsend.at[p, most], back.at[p, most], br_sem.at[p]).wait()


def put_back(parts, out):
    order = gather_rows(True)
    for p in range(PIECES):
        rows = parts[p].reshape(GROUP * MSG, W)
        moved = jnp.dot(order, rows, preferred_element_type=F32).astype(BF16)
        out[:, 0, :, p * W : (p + 1) * W] = moved.reshape(ROWS, MSG, W)


def on_device(ensemble_obs, obs_values, obs_index, obs_count, loc_weight, state):
    any_space = pl.BlockSpec(memory_space=pl.ANY)
    vmem = pl.BlockSpec(memory_space=pltpu.VMEM)
    smem = pl.BlockSpec(memory_space=pltpu.SMEM)
    dma = pltpu.SemaphoreType.DMA
    back = pl.pallas_call(
        exchange,
        name="exchange",
        out_shape=jax.ShapeDtypeStruct((PIECES, PEERS, MSG, W), BF16),
        in_specs=[any_space, vmem, vmem, vmem, smem, vmem],
        out_specs=any_space,
        scratch_shapes=[
            pltpu.VMEM((ROWS, PEERS * BLKS, CELLS), BF16),
            pltpu.VMEM((PIECES, PEERS, MSG, W), BF16),
            pltpu.VMEM((PIECES, PEERS, MSG, W), BF16),
            pltpu.VMEM((PIECES, PEERS, MSG, W), BF16),
            pltpu.VMEM((PEERS, MSG, RIM), BF16),
            pltpu.VMEM((PEERS, MSG, RIM), BF16),
            pltpu.VMEM((2, K + 16, RIM), BF16),
            pltpu.VMEM((2, K + 16, RIM), BF16),
            pltpu.VMEM((K, POOL), BF16),
            pltpu.VMEM((BLKS, K, POOL), BF16),
            pltpu.VMEM((3, K, K), F32),
            pltpu.VMEM((BLKS, K, POOL), BF16),
            pltpu.VMEM((PEERS, MSG, POOL), F32),
            pltpu.VMEM((BLKS * K, BLKS * K), BF16),
            pltpu.VMEM((BLKS * K, W), BF16),
            dma((PIECES,)), dma((PIECES,)), dma((PIECES,)), dma((PIECES,)),
            dma((PIECES,)), dma((PIECES,)), dma((PIECES,)),
            dma, dma, dma, dma((2,)), dma((2,)),
        ],
        compiler_params=pltpu.CompilerParams(
            collective_id=0, has_side_effects=True, vmem_limit_bytes=56 << 20
        ),
    )(
        state,
        ensemble_obs.reshape(ROWS, PEERS * 2 * RIM),
        obs_values.reshape(2, 2 * RIM),
        obs_index.reshape(BLKS, 512),
        obs_count,
        loc_weight.reshape(BLKS, 512),
    )
    return pl.pallas_call(
        put_back,
        name="put_back",
        grid=(GROUPS,),
        out_shape=jax.ShapeDtypeStruct(state.shape, BF16),
        in_specs=[pl.BlockSpec((PIECES, GROUP, MSG, W), lambda g: (0, g, 0, 0))],
        out_specs=pl.BlockSpec((ROWS, 1, MSG, CELLS), lambda g: (0, 0, g, 0)),
    )(back)


def solution(mesh):
    placed = (
        P("member", "slab", None),
        P(None, "slab", "member"),
        P("slab", "member", None),
        P("slab", "member"),
        P("slab", "member", None),
        P("member", "slab", None, None),
    )
    return jax.shard_map(
        on_device,
        mesh=mesh,
        in_specs=placed,
        out_specs=P("member", "slab", None, None),
        check_vma=False,
    )
```

```python
import functools

import jax
import jax.numpy as jnp
from jax import lax
from jax.experimental import pallas as pl
from jax.experimental.pallas import tpu as pltpu
from jax.sharding import PartitionSpec as P

MESH = pl.DeviceIdType.MESH
F32 = jnp.float32
BF16 = jnp.bfloat16
HIGHEST = lax.Precision.HIGHEST

PEERS = 64
SLABS = 4
ROWS = 8
K = 512
BLKS = 2
MSG = BLKS * ROWS
CELLS = 2048
PIECES = 4
W = CELLS // PIECES
RIM = 256
POOL = 1024
GROUP = 8
GROUPS = PEERS // GROUP


def nt(a, b, precision=None):
    return lax.dot_general(
        a, b, (((1,), (1,)), ((), ())), precision=precision, preferred_element_type=F32
    )


def mm(a, b):
    return jnp.dot(a, b, precision=HIGHEST, preferred_element_type=F32)


def iota(shape, axis):
    return lax.broadcasted_iota(jnp.int32, shape, axis)


def split3(row, width):
    full = jnp.broadcast_to(row, (16, width))
    high = full.astype(BF16).astype(F32)
    rest = full - high
    mid = rest.astype(BF16).astype(F32)
    low = rest - mid
    r = iota((16, width), 0)
    rows = jnp.where(r == 0, high, jnp.where(r == 1, mid, jnp.where(r == 2, low, 0.0)))
    return rows.astype(BF16)


def gather_rows(inverse):
    n = GROUP * MSG
    out, src = iota((n, n), 0), iota((n, n), 1)
    if inverse:
        out, src = src, out
    wanted = (out % ROWS) * MSG + out // ROWS
    return jnp.where(src == wanted, 1.0, 0.0).astype(BF16)


def exchange(
    state, obs_in, vals_in, idx_in, cnt_in, loc_in, out,
    obs, vals, idx, loc, cnt, stage, fsend, frecv, bsend, back, osend, orecv, hsend, hrecv,
    pert, wgt, mats, expand, tbigf, tbig, spert,
    in_sem, st_sem, fs_sem, fr_sem, fl_sem, bs_sem, br_sem,
    os_sem, or_sem, ol_sem, hs_sem, hr_sem,
):
    me = lax.axis_index("member")
    slab = lax.axis_index("slab")
    right = lax.rem(slab + 1, SLABS)
    left = lax.rem(slab + SLABS - 1, SLABS)

    barrier = pltpu.get_barrier_semaphore()

    def greet(i, carry):
        pl.semaphore_signal(
            barrier, inc=1, device_id={"member": lax.rem(me + 27 * i, PEERS)}, device_id_type=MESH
        )
        return carry

    lax.fori_loop(1, PEERS, greet, 0, unroll=7)
    for neighbour in (left, right):
        pl.semaphore_signal(barrier, inc=1, device_id={"slab": neighbour}, device_id_type=MESH)

    fetches = [
        pltpu.make_async_copy(source, target, in_sem.at[n])
        for n, (source, target) in enumerate(
            ((obs_in, obs), (vals_in, vals), (idx_in, idx), (loc_in, loc), (cnt_in, cnt))
        )
    ]
    for fetch in fetches:
        fetch.start()

    def stage_copy(p):
        cols = pl.ds(p * W, W)
        return pltpu.make_async_copy(
            state.at[:, 0, :, cols], stage.at[:, :, cols], st_sem.at[p]
        )

    for p in range(PIECES):
        stage_copy(p).start()
    fetches[0].wait()
    pl.semaphore_wait(barrier, PEERS - 1 + 2)

    def message(r):
        a = obs[:, pl.ds(pl.multiple_of(r * 2 * RIM, 2 * RIM), RIM)].astype(F32)
        b = obs[:, pl.ds(pl.multiple_of(r * 2 * RIM + RIM, RIM), RIM)].astype(F32)
        osend[r] = jnp.concatenate([a, b], axis=0).astype(BF16)

    def send_obs(i, carry):
        d = lax.rem(me + 27 * i, PEERS)
        message(d)
        pltpu.make_async_remote_copy(
            src_ref=osend.at[d], dst_ref=orecv.at[me], send_sem=os_sem, recv_sem=or_sem,
            device_id={"member": d}, device_id_type=MESH,
        ).start()
        return carry

    lax.fori_loop(1, PEERS, send_obs, 0)
    message(me)
    own_obs = pltpu.make_async_copy(osend.at[me], orecv.at[me], ol_sem)
    own_obs.start()
    for fetch in fetches[1:]:
        fetch.wait()

    def forward(p):
        stage_copy(p).wait()
        cols = pl.ds(p * W, W)

        def group(i, carry):
            g = lax.rem(me // GROUP + i, GROUPS)
            first = pl.multiple_of(g * GROUP, GROUP)
            rows = stage[:, pl.ds(pl.multiple_of(g * MSG, MSG), MSG), cols]
            moved = jnp.dot(
                gather_rows(False), rows.reshape(GROUP * MSG, W), preferred_element_type=F32
            )
            fsend[p, pl.ds(first, GROUP)] = moved.astype(BF16).reshape(GROUP, MSG, W)

            def one(j, inner):
                d = first + j

                @pl.when(d != me)
                def _():
                    pltpu.make_async_remote_copy(
                        src_ref=fsend.at[p, d], dst_ref=frecv.at[p, me],
                        send_sem=fs_sem.at[p], recv_sem=fr_sem.at[p],
                        device_id={"member": d}, device_id_type=MESH,
                    ).start()

                return inner

            lax.fori_loop(0, GROUP, one, 0)
            return carry

        lax.fori_loop(0, GROUPS, group, 0)
        pltpu.make_async_copy(fsend.at[p, me], frecv.at[p, me], fl_sem.at[p]).start()

    forward(0)

    own_obs.wait()
    most = pl.ds(0, PEERS - 1)
    pltpu.make_async_copy(osend.at[most], orecv.at[most], or_sem).wait()

    def halves(i, carry):
        x = orecv[pl.ds(i * 8, 8)].astype(F32)
        rows = pl.ds(pl.multiple_of(i * 64, 64), 64)
        hsend[1, rows] = x[:, :ROWS].reshape(64, RIM).astype(BF16)
        hsend[0, rows] = x[:, ROWS:].reshape(64, RIM).astype(BF16)
        return carry

    lax.fori_loop(0, 8, halves, 0)
    v = vals[...].astype(F32)
    for side, at in ((1, 0), (0, RIM)):
        r = iota((16, RIM), 0)
        first, second = v[0:1, at : at + RIM], v[1:2, at : at + RIM]
        hsend[side, K : K + 16] = jnp.where(
            r == 0, first, jnp.where(r == 1, second, 0.0)
        ).astype(BF16)
    halos = [
        pltpu.make_async_remote_copy(
            src_ref=hsend.at[side], dst_ref=hrecv.at[side],
            send_sem=hs_sem.at[side], recv_sem=hr_sem.at[side],
            device_id={"slab": to}, device_id_type=MESH,
        )
        for side, to in ((0, right), (1, left))
    ]
    for halo in halos:
        halo.start()

    for p in range(1, PIECES):
        forward(p)

    def fill_expand(i, carry):
        j = iota((64, POOL), 0) + i * 64
        c = iota((64, POOL), 1)
        rows = pl.ds(pl.multiple_of(i * 64, 64), 64)
        for b in range(BLKS):
            at = (j // ROWS) * MSG + b * ROWS + j % ROWS
            expand[b, rows] = jnp.where(c == at, 1.0, 0.0).astype(BF16)
        return carry

    lax.fori_loop(0, K // 64, fill_expand, 0)

    for halo in halos:
        halo.wait()

    departs, inverses = [], []
    for q, ref in enumerate((hrecv.at[0], hsend.at[1], hsend.at[0], hrecv.at[1])):
        x = ref[:K].astype(F32)
        mean = jnp.sum(x, axis=0, keepdims=True) * (1.0 / K)
        pert[:, q * RIM : (q + 1) * RIM] = (x - mean).astype(BF16)
        tail = ref[K : K + 16].astype(F32)
        departs.append(tail[0:1] - mean)
        inverses.append(tail[1:2])
    depart = split3(jnp.concatenate(departs, axis=1), POOL)

    diagonal = iota((K, K), 0) == iota((K, K), 1)
    for b in range(BLKS):
        row = idx[b : b + 1, :]
        slot = iota((1, 512), 1)
        local = jnp.where(slot < cnt[0, b], loc[b : b + 1, :], 0.0)
        local = split3(local, 512)
        for q in range(4):
            hit = iota((RIM, 512), 0) + q * RIM == row
            hit = jnp.where(hit, 1.0, 0.0).astype(BF16)
            total = nt(local, hit)
            weight = inverses[q] * (total[0:1] + total[1:2] + total[2:3])
            cols = slice(q * RIM, (q + 1) * RIM)
            wgt[b, :, cols] = (pert[:, cols].astype(F32) * weight).astype(BF16)

    def transform(b, carry):
        weighted = wgt[b]
        drive = nt(depart, weighted)
        drive = jnp.broadcast_to(drive[0:1] + drive[1:2] + drive[2:3], (8, K))
        gram = nt(pert[...], weighted) + jnp.where(diagonal, K - 1.0, 0.0)
        scale = jnp.sum(gram * gram, axis=1, keepdims=True)
        scale = jnp.sqrt(jnp.sum(scale, axis=0, keepdims=True))
        matrix = gram * (1.0 / scale)
        factor = jnp.where(diagonal, 1.5, 0.0) - 0.5 * matrix
        mats[1] = factor
        mats[0] = mm(matrix, factor)
        mats[2] = jnp.where(diagonal, 1.5, 0.0) - 0.5 * mm(mats[1], mats[0])
        mats[0] = mm(mats[0], mats[2])
        mats[1] = mm(mats[2], mats[1])
        mats[2] = jnp.where(diagonal, 1.5, 0.0) - 0.5 * mm(mats[1], mats[0])
        mats[0] = mm(mats[2], mats[1])
        inverse = mats[0]
        inner = nt(drive, inverse, HIGHEST)
        shift = nt(inner, inverse, HIGHEST)[0:1] / scale
        spread = jnp.sqrt((K - 1.0) / scale)
        mats[1] = spread * inverse.T + shift

        def widen(i, inner_carry):
            rows = mats[1, pl.ds(pl.multiple_of(i * 128, 128), 128)].astype(BF16)
            wide = jnp.dot(rows, expand[b], preferred_element_type=F32)
            at = pl.ds(pl.multiple_of(b * ROWS, ROWS), ROWS)
            tbigf[pl.ds(i * 16, 16), at] = wide.reshape(16, ROWS, POOL)
            return inner_carry

        lax.fori_loop(0, 4, widen, 0)
        return carry

    lax.fori_loop(0, BLKS, transform, 0)

    def narrow(i, carry):
        rows = pl.ds(pl.multiple_of(i * 128, 128), 128)
        tbig[rows] = tbigf[pl.ds(i * 8, 8)].reshape(128, POOL).astype(BF16)
        return carry

    lax.fori_loop(0, 8, narrow, 0)

    for p in range(PIECES):
        pltpu.make_async_copy(fsend.at[p, me], frecv.at[p, me], fl_sem.at[p]).wait()
        pltpu.make_async_copy(fsend.at[p, most], frecv.at[p, most], fr_sem.at[p]).wait()

        def add_up(i, total):
            x = frecv[p, pl.ds(i * 4, 4)].astype(F32)
            return total + jnp.sum(x, axis=0)

        total = lax.fori_loop(0, 16, add_up, jnp.zeros((MSG, W), F32))
        means = [
            jnp.sum(total[b * ROWS : (b + 1) * ROWS], axis=0, keepdims=True) * (1.0 / K)
            for b in range(BLKS)
        ]
        mean = jnp.concatenate([jnp.broadcast_to(m, (ROWS, W)) for m in means], axis=0)

        def less_mean(i, carry):
            x = frecv[p, pl.ds(i * 4, 4)].astype(F32) - mean[None]
            spert[pl.ds(pl.multiple_of(i * 64, 64), 64)] = x.reshape(64, W).astype(BF16)
            return carry

        lax.fori_loop(0, 16, less_mean, 0)

        def apply(i, carry):
            part = lax.rem(me // 16 + i, 4)
            rows = tbig[pl.ds(pl.multiple_of(part * 256, 256), 256)]
            moved = jnp.dot(rows, spert[...], preferred_element_type=F32)
            new = moved.reshape(16, MSG, W) + mean[None]
            first = pl.multiple_of(part * 16, 16)
            bsend[p, pl.ds(first, 16)] = new.astype(BF16)

            def one(j, inner):
                d = first + lax.rem(j * 7 + me, 16)

                @pl.when(d != me)
                def _():
                    pltpu.make_async_remote_copy(
                        src_ref=bsend.at[p, d], dst_ref=back.at[p, me],
                        send_sem=bs_sem.at[p], recv_sem=br_sem.at[p, me // GROUP],
                        device_id={"member": d}, device_id_type=MESH,
                    ).start()

                return inner

            lax.fori_loop(0, 16, one, 0)
            return carry

        lax.fori_loop(0, 4, apply, 0)
        pltpu.make_async_copy(bsend.at[p, me], back.at[p, me], br_sem.at[p, me // GROUP]).start()

    for p in range(PIECES):

        def place(i, carry):
            y = lax.rem(me // 16 + 4 - i // 2, 4)
            g = y * 2 + lax.rem(i, 2)
            some = pl.ds(pl.multiple_of(g * GROUP, GROUP), GROUP)
            pltpu.make_async_copy(bsend.at[p, some], back.at[p, some], br_sem.at[p, g]).wait()
            moved = jnp.dot(
                gather_rows(True), back[p, some].reshape(GROUP * MSG, W), preferred_element_type=F32
            )
            rows = pl.ds(pl.multiple_of(g * MSG, MSG), MSG)
            out[:, 0, rows, p * W : (p + 1) * W] = moved.astype(BF16).reshape(ROWS, MSG, W)
            return carry

        lax.fori_loop(0, GROUPS, place, 0)

    pltpu.make_async_copy(osend.at[most], orecv.at[most], os_sem).wait()
    for p in range(PIECES):
        pltpu.make_async_copy(fsend.at[p, most], frecv.at[p, most], fs_sem.at[p]).wait()
        pltpu.make_async_copy(bsend.at[p, most], back.at[p, most], bs_sem.at[p]).wait()


def on_device(ensemble_obs, obs_values, obs_index, obs_count, loc_weight, state):
    any_space = pl.BlockSpec(memory_space=pl.ANY)
    vmem = pltpu.VMEM
    dma = pltpu.SemaphoreType.DMA

    def in_hbm(array):
        return pltpu.with_memory_space_constraint(array, pltpu.HBM)

    return pl.pallas_call(
        exchange,
        name="exchange",
        out_shape=vmem(state.shape, BF16),
        in_specs=[any_space] * 6,
        out_specs=pl.BlockSpec(memory_space=vmem),
        scratch_shapes=[
            vmem((ROWS, PEERS * 2 * RIM), BF16),
            vmem((2, 2 * RIM), BF16),
            vmem((BLKS, 512), jnp.int32),
            vmem((BLKS, 512), F32),
            pltpu.SMEM((1, BLKS), jnp.int32),
            vmem((ROWS, PEERS * BLKS, CELLS), BF16),
            vmem((PIECES, PEERS, MSG, W), BF16),
            vmem((PIECES, PEERS, MSG, W), BF16),
            vmem((PIECES, PEERS, MSG, W), BF16),
            vmem((PIECES, PEERS, MSG, W), BF16),
            vmem((PEERS, MSG, RIM), BF16),
            vmem((PEERS, MSG, RIM), BF16),
            vmem((2, K + 16, RIM), BF16),
            vmem((2, K + 16, RIM), BF16),
            vmem((K, POOL), BF16),
            vmem((BLKS, K, POOL), BF16),
            vmem((3, K, K), F32),
            vmem((BLKS, K, POOL), BF16),
            vmem((PEERS, MSG, POOL), F32),
            vmem((BLKS * K, BLKS * K), BF16),
            vmem((BLKS * K, W), BF16),
            dma((5,)), dma((PIECES,)), dma((PIECES,)), dma((PIECES,)), dma((PIECES,)),
            dma((PIECES,)), dma((PIECES, GROUPS)),
            dma, dma, dma, dma((2,)), dma((2,)),
        ],
        compiler_params=pltpu.CompilerParams(
            collective_id=0, has_side_effects=True, vmem_limit_bytes=48 << 20
        ),
    )(
        in_hbm(state),
        in_hbm(ensemble_obs.reshape(ROWS, PEERS * 2 * RIM)),
        in_hbm(obs_values.reshape(2, 2 * RIM)),
        in_hbm(obs_index.reshape(BLKS, 512)),
        in_hbm(obs_count),
        in_hbm(loc_weight.reshape(BLKS, 512)),
    )


def solution(mesh):
    placed = (
        P("member", "slab", None),
        P(None, "slab", "member"),
        P("slab", "member", None),
        P("slab", "member"),
        P("slab", "member", None),
        P("member", "slab", None, None),
    )
    return jax.shard_map(
        on_device,
        mesh=mesh,
        in_specs=placed,
        out_specs=P("member", "slab", None, None),
        check_vma=False,
    )
```

```python
import functools

import jax
import jax.numpy as jnp
from jax import lax
from jax.experimental import pallas as pl
from jax.experimental.pallas import tpu as pltpu
from jax.sharding import PartitionSpec as P

MESH = pl.DeviceIdType.MESH
F32 = jnp.float32
BF16 = jnp.bfloat16
HIGHEST = lax.Precision.HIGHEST

PEERS = 64
SLABS = 4
ROWS = 8
K = 512
BLKS = 2
MSG = BLKS * ROWS
CELLS = 2048
PIECES = 4
W = CELLS // PIECES
RIM = 256
POOL = 1024
GROUP = 8
GROUPS = PEERS // GROUP


def nt(a, b, precision=None):
    return lax.dot_general(
        a, b, (((1,), (1,)), ((), ())), precision=precision, preferred_element_type=F32
    )


def mm(a, b):
    return jnp.dot(a, b, precision=HIGHEST, preferred_element_type=F32)


def iota(shape, axis):
    return lax.broadcasted_iota(jnp.int32, shape, axis)


def split3(row, width):
    full = jnp.broadcast_to(row, (16, width))
    high = full.astype(BF16).astype(F32)
    rest = full - high
    mid = rest.astype(BF16).astype(F32)
    low = rest - mid
    r = iota((16, width), 0)
    rows = jnp.where(r == 0, high, jnp.where(r == 1, mid, jnp.where(r == 2, low, 0.0)))
    return rows.astype(BF16)


def gather_rows(inverse):
    n = GROUP * MSG
    out, src = iota((n, n), 0), iota((n, n), 1)
    if inverse:
        out, src = src, out
    wanted = (out % ROWS) * MSG + out // ROWS
    return jnp.where(src == wanted, 1.0, 0.0).astype(BF16)


def exchange(
    state, obs_in, vals_in, idx_in, cnt_in, loc_in, out,
    obs, vals, idx, loc, cnt, stage, fsend, frecv, bsend, back, osend, orecv, hsend, hrecv,
    pert, wgt, mats, expand, tbigf, tbig, spert,
    in_sem, st_sem, fs_sem, fr_sem, fl_sem, bs_sem, br_sem,
    os_sem, or_sem, ol_sem, hs_sem, hr_sem, relay,
):
    me = lax.axis_index("member")
    slab = lax.axis_index("slab")
    right = lax.rem(slab + 1, SLABS)
    left = lax.rem(slab + SLABS - 1, SLABS)

    barrier = pltpu.get_barrier_semaphore()

    corner = [
        lax.rem(me // 16 + n // 2, 4) * 16 + lax.rem(me + n, 2) for n in range(8)
    ]

    def plane(dz):
        at = lax.rem(me // 2 + dz, 8) * 2
        return [corner[n] + at for n in range(8)]

    up, down = plane(1)[0], plane(7)[0]

    def signal(semaphore, member):
        pl.semaphore_signal(
            semaphore, inc=1, device_id={"member": member}, device_id_type=MESH
        )

    for d in plane(1) + plane(7) + plane(0)[1:]:
        signal(barrier, d)
    for neighbour in (left, right):
        pl.semaphore_signal(barrier, inc=1, device_id={"slab": neighbour}, device_id_type=MESH)

    fetches = [
        pltpu.make_async_copy(source, target, in_sem.at[n])
        for n, (source, target) in enumerate(
            ((obs_in, obs), (vals_in, vals), (idx_in, idx), (loc_in, loc), (cnt_in, cnt))
        )
    ]
    for fetch in fetches:
        fetch.start()

    def stage_copy(p):
        cols = pl.ds(p * W, W)
        return pltpu.make_async_copy(
            state.at[:, 0, :, cols], stage.at[:, :, cols], st_sem.at[p]
        )

    for p in range(PIECES):
        stage_copy(p).start()
    fetches[0].wait()
    pl.semaphore_wait(barrier, 8 + 8 + 7 + 2)

    def message(r):
        a = obs[:, pl.ds(pl.multiple_of(r * 2 * RIM, 2 * RIM), RIM)].astype(F32)
        b = obs[:, pl.ds(pl.multiple_of(r * 2 * RIM + RIM, RIM), RIM)].astype(F32)
        osend[r] = jnp.concatenate([a, b], axis=0).astype(BF16)

    def send_obs(d):
        message(d)
        pltpu.make_async_remote_copy(
            src_ref=osend.at[d], dst_ref=orecv.at[me], send_sem=os_sem, recv_sem=or_sem,
            device_id={"member": d}, device_id_type=MESH,
        ).start()

    for far in range(1, 5):
        if far in (2, 3):
            pl.semaphore_wait(relay.at[far - 2, 0], 1)
        if far > 1:
            pl.semaphore_wait(relay.at[far - 2, 1], 1)
        if far < 4:
            signal(relay.at[far - 1, 1], up)
        if far < 3:
            signal(relay.at[far - 1, 0], down)
        reach = {1: plane(1) + plane(7), 4: plane(4)}.get(far, plane(far) + plane(8 - far))
        for d in reach + (plane(0)[1:] if far == 1 else []):
            send_obs(d)
    message(me)
    own_obs = pltpu.make_async_copy(osend.at[me], orecv.at[me], ol_sem)
    own_obs.start()
    for fetch in fetches[1:]:
        fetch.wait()

    def forward(p):
        stage_copy(p).wait()
        cols = pl.ds(p * W, W)

        def group(i, carry):
            g = lax.rem(me // GROUP + i, GROUPS)
            first = pl.multiple_of(g * GROUP, GROUP)
            rows = stage[:, pl.ds(pl.multiple_of(g * MSG, MSG), MSG), cols]
            moved = jnp.dot(
                gather_rows(False), rows.reshape(GROUP * MSG, W), preferred_element_type=F32
            )
            fsend[p, pl.ds(first, GROUP)] = moved.astype(BF16).reshape(GROUP, MSG, W)

            def one(j, inner):
                d = first + j

                @pl.when(d != me)
                def _():
                    pltpu.make_async_remote_copy(
                        src_ref=fsend.at[p, d], dst_ref=frecv.at[p, me],
                        send_sem=fs_sem.at[p], recv_sem=fr_sem.at[p],
                        device_id={"member": d}, device_id_type=MESH,
                    ).start()

                return inner

            lax.fori_loop(0, GROUP, one, 0)
            return carry

        lax.fori_loop(0, GROUPS, group, 0)
        pltpu.make_async_copy(fsend.at[p, me], frecv.at[p, me], fl_sem.at[p]).start()

    forward(0)

    own_obs.wait()
    most = pl.ds(0, PEERS - 1)
    pltpu.make_async_copy(osend.at[most], orecv.at[most], or_sem).wait()

    def halves(i, carry):
        x = orecv[pl.ds(i * 8, 8)].astype(F32)
        rows = pl.ds(pl.multiple_of(i * 64, 64), 64)
        hsend[1, rows] = x[:, :ROWS].reshape(64, RIM).astype(BF16)
        hsend[0, rows] = x[:, ROWS:].reshape(64, RIM).astype(BF16)
        return carry

    lax.fori_loop(0, 8, halves, 0)
    v = vals[...].astype(F32)
    for side, at in ((1, 0), (0, RIM)):
        r = iota((16, RIM), 0)
        first, second = v[0:1, at : at + RIM], v[1:2, at : at + RIM]
        hsend[side, K : K + 16] = jnp.where(
            r == 0, first, jnp.where(r == 1, second, 0.0)
        ).astype(BF16)
    halos = [
        pltpu.make_async_remote_copy(
            src_ref=hsend.at[side], dst_ref=hrecv.at[side],
            send_sem=hs_sem.at[side], recv_sem=hr_sem.at[side],
            device_id={"slab": to}, device_id_type=MESH,
        )
        for side, to in ((0, right), (1, left))
    ]
    for halo in halos:
        halo.start()

    for p in range(1, PIECES):
        forward(p)

    def fill_expand(i, carry):
        j = iota((64, POOL), 0) + i * 64
        c = iota((64, POOL), 1)
        rows = pl.ds(pl.multiple_of(i * 64, 64), 64)
        for b in range(BLKS):
            at = (j // ROWS) * MSG + b * ROWS + j % ROWS
            expand[b, rows] = jnp.where(c == at, 1.0, 0.0).astype(BF16)
        return carry

    lax.fori_loop(0, K // 64, fill_expand, 0)

    for halo in halos:
        halo.wait()

    departs, inverses = [], []
    for q, ref in enumerate((hrecv.at[0], hsend.at[1], hsend.at[0], hrecv.at[1])):
        x = ref[:K].astype(F32)
        mean = jnp.sum(x, axis=0, keepdims=True) * (1.0 / K)
        pert[:, q * RIM : (q + 1) * RIM] = (x - mean).astype(BF16)
        tail = ref[K : K + 16].astype(F32)
        departs.append(tail[0:1] - mean)
        inverses.append(tail[1:2])
    depart = split3(jnp.concatenate(departs, axis=1), POOL)

    diagonal = iota((K, K), 0) == iota((K, K), 1)
    for b in range(BLKS):
        row = idx[b : b + 1, :]
        slot = iota((1, 512), 1)
        local = jnp.where(slot < cnt[0, b], loc[b : b + 1, :], 0.0)
        local = split3(local, 512)
        for q in range(4):
            hit = iota((RIM, 512), 0) + q * RIM == row
            hit = jnp.where(hit, 1.0, 0.0).astype(BF16)
            total = nt(local, hit)
            weight = inverses[q] * (total[0:1] + total[1:2] + total[2:3])
            cols = slice(q * RIM, (q + 1) * RIM)
            wgt[b, :, cols] = (pert[:, cols].astype(F32) * weight).astype(BF16)

    def transform(b, carry):
        weighted = wgt[b]
        drive = nt(depart, weighted)
        drive = jnp.broadcast_to(drive[0:1] + drive[1:2] + drive[2:3], (8, K))
        gram = nt(pert[...], weighted) + jnp.where(diagonal, K - 1.0, 0.0)
        scale = jnp.sum(gram * gram, axis=1, keepdims=True)
        scale = jnp.sqrt(jnp.sum(scale, axis=0, keepdims=True))
        matrix = gram * (1.0 / scale)
        factor = jnp.where(diagonal, 1.5, 0.0) - 0.5 * matrix
        mats[1] = factor
        mats[0] = mm(matrix, factor)
        mats[2] = jnp.where(diagonal, 1.5, 0.0) - 0.5 * mm(mats[1], mats[0])
        mats[0] = mm(mats[0], mats[2])
        mats[1] = mm(mats[2], mats[1])
        mats[2] = jnp.where(diagonal, 1.5, 0.0) - 0.5 * mm(mats[1], mats[0])
        mats[0] = mm(mats[2], mats[1])
        inverse = mats[0]
        inner = nt(drive, inverse, HIGHEST)
        shift = nt(inner, inverse, HIGHEST)[0:1] / scale
        spread = jnp.sqrt((K - 1.0) / scale)
        mats[1] = spread * inverse.T + shift

        def widen(i, inner_carry):
            rows = mats[1, pl.ds(pl.multiple_of(i * 128, 128), 128)].astype(BF16)
            wide = jnp.dot(rows, expand[b], preferred_element_type=F32)
            at = pl.ds(pl.multiple_of(b * ROWS, ROWS), ROWS)
            tbigf[pl.ds(i * 16, 16), at] = wide.reshape(16, ROWS, POOL)
            return inner_carry

        lax.fori_loop(0, 4, widen, 0)
        return carry

    lax.fori_loop(0, BLKS, transform, 0)

    def narrow(i, carry):
        rows = pl.ds(pl.multiple_of(i * 128, 128), 128)
        tbig[rows] = tbigf[pl.ds(i * 8, 8)].reshape(128, POOL).astype(BF16)
        return carry

    lax.fori_loop(0, 8, narrow, 0)

    for p in range(PIECES):
        pltpu.make_async_copy(fsend.at[p, me], frecv.at[p, me], fl_sem.at[p]).wait()
        pltpu.make_async_copy(fsend.at[p, most], frecv.at[p, most], fr_sem.at[p]).wait()

        def add_up(i, total):
            x = frecv[p, pl.ds(i * 4, 4)].astype(F32)
            return total + jnp.sum(x, axis=0)

        total = lax.fori_loop(0, 16, add_up, jnp.zeros((MSG, W), F32))
        means = [
            jnp.sum(total[b * ROWS : (b + 1) * ROWS], axis=0, keepdims=True) * (1.0 / K)
            for b in range(BLKS)
        ]
        mean = jnp.concatenate([jnp.broadcast_to(m, (ROWS, W)) for m in means], axis=0)

        def less_mean(i, carry):
            x = frecv[p, pl.ds(i * 4, 4)].astype(F32) - mean[None]
            spert[pl.ds(pl.multiple_of(i * 64, 64), 64)] = x.reshape(64, W).astype(BF16)
            return carry

        lax.fori_loop(0, 16, less_mean, 0)

        def apply(i, carry):
            part = lax.rem(me // 16 + i, 4)
            rows = tbig[pl.ds(pl.multiple_of(part * 256, 256), 256)]
            moved = jnp.dot(rows, spert[...], preferred_element_type=F32)
            new = moved.reshape(16, MSG, W) + mean[None]
            first = pl.multiple_of(part * 16, 16)
            bsend[p, pl.ds(first, 16)] = new.astype(BF16)

            def one(j, inner):
                d = first + lax.rem(j * 7 + me, 16)

                @pl.when(d != me)
                def _():
                    pltpu.make_async_remote_copy(
                        src_ref=bsend.at[p, d], dst_ref=back.at[p, me],
                        send_sem=bs_sem.at[p], recv_sem=br_sem.at[p, me // GROUP],
                        device_id={"member": d}, device_id_type=MESH,
                    ).start()

                return inner

            lax.fori_loop(0, 16, one, 0)
            return carry

        lax.fori_loop(0, 4, apply, 0)
        pltpu.make_async_copy(bsend.at[p, me], back.at[p, me], br_sem.at[p, me // GROUP]).start()

    for p in range(PIECES):

        def place(i, carry):
            y = lax.rem(me // 16 + 4 - i // 2, 4)
            g = y * 2 + lax.rem(i, 2)
            some = pl.ds(pl.multiple_of(g * GROUP, GROUP), GROUP)
            pltpu.make_async_copy(bsend.at[p, some], back.at[p, some], br_sem.at[p, g]).wait()
            moved = jnp.dot(
                gather_rows(True), back[p, some].reshape(GROUP * MSG, W), preferred_element_type=F32
            )
            rows = pl.ds(pl.multiple_of(g * MSG, MSG), MSG)
            out[:, 0, rows, p * W : (p + 1) * W] = moved.astype(BF16).reshape(ROWS, MSG, W)
            return carry

        lax.fori_loop(0, GROUPS, place, 0)

    pltpu.make_async_copy(osend.at[most], orecv.at[most], os_sem).wait()
    for p in range(PIECES):
        pltpu.make_async_copy(fsend.at[p, most], frecv.at[p, most], fs_sem.at[p]).wait()
        pltpu.make_async_copy(bsend.at[p, most], back.at[p, most], bs_sem.at[p]).wait()


def on_device(ensemble_obs, obs_values, obs_index, obs_count, loc_weight, state):
    any_space = pl.BlockSpec(memory_space=pl.ANY)
    vmem = pltpu.VMEM
    dma = pltpu.SemaphoreType.DMA

    def in_hbm(array):
        return pltpu.with_memory_space_constraint(array, pltpu.HBM)

    return pl.pallas_call(
        exchange,
        name="exchange",
        out_shape=vmem(state.shape, BF16),
        in_specs=[any_space] * 6,
        out_specs=pl.BlockSpec(memory_space=vmem),
        scratch_shapes=[
            vmem((ROWS, PEERS * 2 * RIM), BF16),
            vmem((2, 2 * RIM), BF16),
            vmem((BLKS, 512), jnp.int32),
            vmem((BLKS, 512), F32),
            pltpu.SMEM((1, BLKS), jnp.int32),
            vmem((ROWS, PEERS * BLKS, CELLS), BF16),
            vmem((PIECES, PEERS, MSG, W), BF16),
            vmem((PIECES, PEERS, MSG, W), BF16),
            vmem((PIECES, PEERS, MSG, W), BF16),
            vmem((PIECES, PEERS, MSG, W), BF16),
            vmem((PEERS, MSG, RIM), BF16),
            vmem((PEERS, MSG, RIM), BF16),
            vmem((2, K + 16, RIM), BF16),
            vmem((2, K + 16, RIM), BF16),
            vmem((K, POOL), BF16),
            vmem((BLKS, K, POOL), BF16),
            vmem((3, K, K), F32),
            vmem((BLKS, K, POOL), BF16),
            vmem((PEERS, MSG, POOL), F32),
            vmem((BLKS * K, BLKS * K), BF16),
            vmem((BLKS * K, W), BF16),
            dma((5,)), dma((PIECES,)), dma((PIECES,)), dma((PIECES,)), dma((PIECES,)),
            dma((PIECES,)), dma((PIECES, GROUPS)),
            dma, dma, dma, dma((2,)), dma((2,)), pltpu.SemaphoreType.REGULAR((3, 2)),
        ],
        compiler_params=pltpu.CompilerParams(
            collective_id=0, has_side_effects=True, vmem_limit_bytes=48 << 20
        ),
    )(
        in_hbm(state),
        in_hbm(ensemble_obs.reshape(ROWS, PEERS * 2 * RIM)),
        in_hbm(obs_values.reshape(2, 2 * RIM)),
        in_hbm(obs_index.reshape(BLKS, 512)),
        in_hbm(obs_count),
        in_hbm(loc_weight.reshape(BLKS, 512)),
    )


def solution(mesh):
    placed = (
        P("member", "slab", None),
        P(None, "slab", "member"),
        P("slab", "member", None),
        P("slab", "member"),
        P("slab", "member", None),
        P("member", "slab", None, None),
    )
    return jax.shard_map(
        on_device,
        mesh=mesh,
        in_specs=placed,
        out_specs=P("member", "slab", None, None),
        check_vma=False,
    )
```

```python
import functools

import jax
import jax.numpy as jnp
from jax import lax
from jax.experimental import pallas as pl
from jax.experimental.pallas import tpu as pltpu
from jax.sharding import PartitionSpec as P

MESH = pl.DeviceIdType.MESH
F32 = jnp.float32
BF16 = jnp.bfloat16
HIGHEST = lax.Precision.HIGHEST

PEERS = 64
SLABS = 4
ROWS = 8
K = 512
BLKS = 2
MSG = BLKS * ROWS
CELLS = 2048
PIECES = 4
W = CELLS // PIECES
RIM = 256
POOL = 1024
GROUP = 8
GROUPS = PEERS // GROUP


def nt(a, b, precision=None):
    return lax.dot_general(
        a, b, (((1,), (1,)), ((), ())), precision=precision, preferred_element_type=F32
    )


def mm(a, b):
    return jnp.dot(a, b, precision=HIGHEST, preferred_element_type=F32)


def iota(shape, axis):
    return lax.broadcasted_iota(jnp.int32, shape, axis)


def split3(row, width):
    full = jnp.broadcast_to(row, (16, width))
    high = full.astype(BF16).astype(F32)
    rest = full - high
    mid = rest.astype(BF16).astype(F32)
    low = rest - mid
    r = iota((16, width), 0)
    rows = jnp.where(r == 0, high, jnp.where(r == 1, mid, jnp.where(r == 2, low, 0.0)))
    return rows.astype(BF16)


def gather_rows(inverse):
    n = GROUP * MSG
    out, src = iota((n, n), 0), iota((n, n), 1)
    if inverse:
        out, src = src, out
    wanted = (out % ROWS) * MSG + out // ROWS
    return jnp.where(src == wanted, 1.0, 0.0).astype(BF16)


def exchange(
    state, obs_in, vals_in, idx_in, cnt_in, loc_in, out,
    obs, vals, idx, loc, cnt, stage, fsend, frecv, bsend, back, osend, orecv, hsend, hrecv,
    pert, wgt, mats, expand, tbigf, tbig, spert,
    in_sem, st_sem, fs_sem, fr_sem, fl_sem, bs_sem, br_sem,
    os_sem, or_sem, ol_sem, hs_sem, hr_sem, relay,
):
    me = lax.axis_index("member")
    slab = lax.axis_index("slab")
    right = lax.rem(slab + 1, SLABS)
    left = lax.rem(slab + SLABS - 1, SLABS)

    barrier = pltpu.get_barrier_semaphore()

    corner = [
        lax.rem(me // 16 + n // 2, 4) * 16 + lax.rem(me + n, 2) for n in range(8)
    ]

    def plane(dz):
        at = lax.rem(me // 2 + dz, 8) * 2
        return [corner[n] + at for n in range(8)]

    up, down = plane(1)[0], plane(7)[0]

    def signal(semaphore, member):
        pl.semaphore_signal(
            semaphore, inc=1, device_id={"member": member}, device_id_type=MESH
        )

    for d in plane(1) + plane(7) + plane(0)[1:]:
        signal(barrier, d)
    for neighbour in (left, right):
        pl.semaphore_signal(barrier, inc=1, device_id={"slab": neighbour}, device_id_type=MESH)

    fetches = [
        pltpu.make_async_copy(source, target, in_sem.at[n])
        for n, (source, target) in enumerate(
            ((obs_in, obs), (vals_in, vals), (idx_in, idx), (loc_in, loc), (cnt_in, cnt))
        )
    ]
    for fetch in fetches:
        fetch.start()

    def stage_copy(p):
        cols = pl.ds(p * W, W)
        return pltpu.make_async_copy(
            state.at[:, 0, :, cols], stage.at[:, :, cols], st_sem.at[p]
        )

    for p in range(PIECES):
        stage_copy(p).start()
    fetches[0].wait()
    pl.semaphore_wait(barrier, 8 + 8 + 7 + 2)

    def message(r):
        a = obs[:, pl.ds(pl.multiple_of(r * 2 * RIM, 2 * RIM), RIM)].astype(F32)
        b = obs[:, pl.ds(pl.multiple_of(r * 2 * RIM + RIM, RIM), RIM)].astype(F32)
        osend[r] = jnp.concatenate([a, b], axis=0).astype(BF16)

    def send_obs(d):
        message(d)
        pltpu.make_async_remote_copy(
            src_ref=osend.at[d], dst_ref=orecv.at[me], send_sem=os_sem, recv_sem=or_sem,
            device_id={"member": d}, device_id_type=MESH,
        ).start()

    for far in range(1, 5):
        if far in (2, 3):
            pl.semaphore_wait(relay.at[far - 2, 0], 1)
        if far > 1:
            pl.semaphore_wait(relay.at[far - 2, 1], 1)
        if far < 4:
            signal(relay.at[far - 1, 1], up)
        if far < 3:
            signal(relay.at[far - 1, 0], down)
        reach = {1: plane(1) + plane(7), 4: plane(4)}.get(far, plane(far) + plane(8 - far))
        for d in reach + (plane(0)[1:] if far == 1 else []):
            send_obs(d)
    message(me)
    own_obs = pltpu.make_async_copy(osend.at[me], orecv.at[me], ol_sem)
    own_obs.start()
    for fetch in fetches[1:]:
        fetch.wait()

    def forward(p):
        stage_copy(p).wait()
        cols = pl.ds(p * W, W)

        def group(i, carry):
            g = lax.rem(me // GROUP + i, GROUPS)
            first = pl.multiple_of(g * GROUP, GROUP)
            rows = stage[:, pl.ds(pl.multiple_of(g * MSG, MSG), MSG), cols]
            moved = jnp.dot(
                gather_rows(False), rows.reshape(GROUP * MSG, W), preferred_element_type=F32
            )
            fsend[p, pl.ds(first, GROUP)] = moved.astype(BF16).reshape(GROUP, MSG, W)

            def one(j, inner):
                d = first + j

                @pl.when(d != me)
                def _():
                    pltpu.make_async_remote_copy(
                        src_ref=fsend.at[p, d], dst_ref=frecv.at[p, me],
                        send_sem=fs_sem.at[p], recv_sem=fr_sem.at[p],
                        device_id={"member": d}, device_id_type=MESH,
                    ).start()

                return inner

            lax.fori_loop(0, GROUP, one, 0)
            return carry

        lax.fori_loop(0, GROUPS, group, 0)
        pltpu.make_async_copy(fsend.at[p, me], frecv.at[p, me], fl_sem.at[p]).start()

    forward(0)

    own_obs.wait()
    most = pl.ds(0, PEERS - 1)
    pltpu.make_async_copy(osend.at[most], orecv.at[most], or_sem).wait()

    def halves(i, carry):
        x = orecv[pl.ds(i * 8, 8)].astype(F32)
        rows = pl.ds(pl.multiple_of(i * 64, 64), 64)
        hsend[1, rows] = x[:, :ROWS].reshape(64, RIM).astype(BF16)
        hsend[0, rows] = x[:, ROWS:].reshape(64, RIM).astype(BF16)
        return carry

    lax.fori_loop(0, 8, halves, 0)
    v = vals[...].astype(F32)
    for side, at in ((1, 0), (0, RIM)):
        r = iota((16, RIM), 0)
        first, second = v[0:1, at : at + RIM], v[1:2, at : at + RIM]
        hsend[side, K : K + 16] = jnp.where(
            r == 0, first, jnp.where(r == 1, second, 0.0)
        ).astype(BF16)
    halos = [
        pltpu.make_async_remote_copy(
            src_ref=hsend.at[side], dst_ref=hrecv.at[side],
            send_sem=hs_sem.at[side], recv_sem=hr_sem.at[side],
            device_id={"slab": to}, device_id_type=MESH,
        )
        for side, to in ((0, right), (1, left))
    ]
    for halo in halos:
        halo.start()

    for p in range(1, PIECES):
        forward(p)

    def fill_expand(i, carry):
        j = iota((64, POOL), 0) + i * 64
        c = iota((64, POOL), 1)
        rows = pl.ds(pl.multiple_of(i * 64, 64), 64)
        for b in range(BLKS):
            at = (j // ROWS) * MSG + b * ROWS + j % ROWS
            expand[b, rows] = jnp.where(c == at, 1.0, 0.0).astype(BF16)
        return carry

    lax.fori_loop(0, K // 64, fill_expand, 0)

    for halo in halos:
        halo.wait()

    departs, inverses = [], []
    for q, ref in enumerate((hrecv.at[0], hsend.at[1], hsend.at[0], hrecv.at[1])):
        x = ref[:K].astype(F32)
        mean = jnp.sum(x, axis=0, keepdims=True) * (1.0 / K)
        pert[:, q * RIM : (q + 1) * RIM] = (x - mean).astype(BF16)
        tail = ref[K : K + 16].astype(F32)
        departs.append(tail[0:1] - mean)
        inverses.append(tail[1:2])
    depart = split3(jnp.concatenate(departs, axis=1), POOL)

    diagonal = iota((K, K), 0) == iota((K, K), 1)
    for b in range(BLKS):
        row = idx[b : b + 1, :]
        slot = iota((1, 512), 1)
        local = jnp.where(slot < cnt[0, b], loc[b : b + 1, :], 0.0)
        local = split3(local, 512)
        for q in range(4):
            hit = iota((RIM, 512), 0) + q * RIM == row
            hit = jnp.where(hit, 1.0, 0.0).astype(BF16)
            total = nt(local, hit)
            weight = inverses[q] * (total[0:1] + total[1:2] + total[2:3])
            cols = slice(q * RIM, (q + 1) * RIM)
            wgt[b, :, cols] = (pert[:, cols].astype(F32) * weight).astype(BF16)

    def transform(b, carry):
        weighted = wgt[b]
        drive = nt(depart, weighted)
        drive = jnp.broadcast_to(drive[0:1] + drive[1:2] + drive[2:3], (8, K))
        gram = nt(pert[...], weighted) + jnp.where(diagonal, K - 1.0, 0.0)
        scale = jnp.sum(gram * gram, axis=1, keepdims=True)
        scale = jnp.sqrt(jnp.sum(scale, axis=0, keepdims=True))
        matrix = gram * (1.0 / scale)
        factor = jnp.where(diagonal, 1.5, 0.0) - 0.5 * matrix
        mats[1] = factor
        mats[0] = mm(matrix, factor)
        mats[2] = jnp.where(diagonal, 1.5, 0.0) - 0.5 * mm(mats[1], mats[0])
        mats[0] = mm(mats[0], mats[2])
        mats[1] = mm(mats[2], mats[1])
        mats[2] = jnp.where(diagonal, 1.5, 0.0) - 0.5 * mm(mats[1], mats[0])
        mats[0] = mm(mats[2], mats[1])
        inverse = mats[0]
        inner = nt(drive, inverse, HIGHEST)
        shift = nt(inner, inverse, HIGHEST)[0:1] / scale
        spread = jnp.sqrt((K - 1.0) / scale)
        mats[1] = spread * inverse.T + shift

        def widen(i, inner_carry):
            rows = mats[1, pl.ds(pl.multiple_of(i * 128, 128), 128)].astype(BF16)
            wide = jnp.dot(rows, expand[b], preferred_element_type=F32)
            at = pl.ds(pl.multiple_of(b * ROWS, ROWS), ROWS)
            tbigf[pl.ds(i * 16, 16), at] = wide.reshape(16, ROWS, POOL)
            return inner_carry

        lax.fori_loop(0, 4, widen, 0)
        return carry

    lax.fori_loop(0, BLKS, transform, 0)

    def narrow(i, carry):
        rows = pl.ds(pl.multiple_of(i * 128, 128), 128)
        tbig[rows] = tbigf[pl.ds(i * 8, 8)].reshape(128, POOL).astype(BF16)
        return carry

    lax.fori_loop(0, 8, narrow, 0)

    for p in range(PIECES):
        pltpu.make_async_copy(fsend.at[p, me], frecv.at[p, me], fl_sem.at[p]).wait()
        pltpu.make_async_copy(fsend.at[p, most], frecv.at[p, most], fr_sem.at[p]).wait()

        def add_up(i, total):
            x = frecv[p, pl.ds(i * 4, 4)].astype(F32)
            return total + jnp.sum(x, axis=0)

        total = lax.fori_loop(0, 16, add_up, jnp.zeros((MSG, W), F32))
        means = [
            jnp.sum(total[b * ROWS : (b + 1) * ROWS], axis=0, keepdims=True) * (1.0 / K)
            for b in range(BLKS)
        ]
        mean = jnp.concatenate([jnp.broadcast_to(m, (ROWS, W)) for m in means], axis=0)

        def less_mean(i, carry):
            x = frecv[p, pl.ds(i * 4, 4)].astype(F32) - mean[None]
            spert[pl.ds(pl.multiple_of(i * 64, 64), 64)] = x.reshape(64, W).astype(BF16)
            return carry

        lax.fori_loop(0, 16, less_mean, 0)

        def apply(i, carry):
            part = lax.rem(me // 16 + 1 + i, 4)
            rows = tbig[pl.ds(pl.multiple_of(part * 256, 256), 256)]
            moved = jnp.dot(rows, spert[...], preferred_element_type=F32)
            new = moved.reshape(16, MSG, W) + mean[None]
            first = pl.multiple_of(part * 16, 16)
            bsend[p, pl.ds(first, 16)] = new.astype(BF16)

            def one(j, inner):
                step = j // 2
                dz = lax.rem(4 + (1 - 2 * lax.rem(step, 2)) * ((step + 1) // 2) + 8, 8)
                d = first + lax.rem(me // 2 + dz, 8) * 2 + lax.rem(j + me, 2)

                @pl.when(d != me)
                def _():
                    pltpu.make_async_remote_copy(
                        src_ref=bsend.at[p, d], dst_ref=back.at[p, me],
                        send_sem=bs_sem.at[p], recv_sem=br_sem.at[p, me // GROUP],
                        device_id={"member": d}, device_id_type=MESH,
                    ).start()

                return inner

            lax.fori_loop(0, 16, one, 0)
            return carry

        lax.fori_loop(0, 4, apply, 0)
        pltpu.make_async_copy(bsend.at[p, me], back.at[p, me], br_sem.at[p, me // GROUP]).start()

    for p in range(PIECES):

        def place(i, carry):
            y = lax.rem(me // 16 + 3 - i // 2, 4)
            g = y * 2 + lax.rem(i, 2)
            some = pl.ds(pl.multiple_of(g * GROUP, GROUP), GROUP)
            pltpu.make_async_copy(bsend.at[p, some], back.at[p, some], br_sem.at[p, g]).wait()
            moved = jnp.dot(
                gather_rows(True), back[p, some].reshape(GROUP * MSG, W), preferred_element_type=F32
            )
            rows = pl.ds(pl.multiple_of(g * MSG, MSG), MSG)
            out[:, 0, rows, p * W : (p + 1) * W] = moved.astype(BF16).reshape(ROWS, MSG, W)
            return carry

        lax.fori_loop(0, GROUPS, place, 0)

    pltpu.make_async_copy(osend.at[most], orecv.at[most], os_sem).wait()
    for p in range(PIECES):
        pltpu.make_async_copy(fsend.at[p, most], frecv.at[p, most], fs_sem.at[p]).wait()
        pltpu.make_async_copy(bsend.at[p, most], back.at[p, most], bs_sem.at[p]).wait()


def on_device(ensemble_obs, obs_values, obs_index, obs_count, loc_weight, state):
    any_space = pl.BlockSpec(memory_space=pl.ANY)
    vmem = pltpu.VMEM
    dma = pltpu.SemaphoreType.DMA

    def in_hbm(array):
        return pltpu.with_memory_space_constraint(array, pltpu.HBM)

    return pl.pallas_call(
        exchange,
        name="exchange",
        out_shape=vmem(state.shape, BF16),
        in_specs=[any_space] * 6,
        out_specs=pl.BlockSpec(memory_space=vmem),
        scratch_shapes=[
            vmem((ROWS, PEERS * 2 * RIM), BF16),
            vmem((2, 2 * RIM), BF16),
            vmem((BLKS, 512), jnp.int32),
            vmem((BLKS, 512), F32),
            pltpu.SMEM((1, BLKS), jnp.int32),
            vmem((ROWS, PEERS * BLKS, CELLS), BF16),
            vmem((PIECES, PEERS, MSG, W), BF16),
            vmem((PIECES, PEERS, MSG, W), BF16),
            vmem((PIECES, PEERS, MSG, W), BF16),
            vmem((PIECES, PEERS, MSG, W), BF16),
            vmem((PEERS, MSG, RIM), BF16),
            vmem((PEERS, MSG, RIM), BF16),
            vmem((2, K + 16, RIM), BF16),
            vmem((2, K + 16, RIM), BF16),
            vmem((K, POOL), BF16),
            vmem((BLKS, K, POOL), BF16),
            vmem((3, K, K), F32),
            vmem((BLKS, K, POOL), BF16),
            vmem((PEERS, MSG, POOL), F32),
            vmem((BLKS * K, BLKS * K), BF16),
            vmem((BLKS * K, W), BF16),
            dma((5,)), dma((PIECES,)), dma((PIECES,)), dma((PIECES,)), dma((PIECES,)),
            dma((PIECES,)), dma((PIECES, GROUPS)),
            dma, dma, dma, dma((2,)), dma((2,)), pltpu.SemaphoreType.REGULAR((3, 2)),
        ],
        compiler_params=pltpu.CompilerParams(
            collective_id=0, has_side_effects=True, vmem_limit_bytes=48 << 20
        ),
    )(
        in_hbm(state),
        in_hbm(ensemble_obs.reshape(ROWS, PEERS * 2 * RIM)),
        in_hbm(obs_values.reshape(2, 2 * RIM)),
        in_hbm(obs_index.reshape(BLKS, 512)),
        in_hbm(obs_count),
        in_hbm(loc_weight.reshape(BLKS, 512)),
    )


def solution(mesh):
    placed = (
        P("member", "slab", None),
        P(None, "slab", "member"),
        P("slab", "member", None),
        P("slab", "member"),
        P("slab", "member", None),
        P("member", "slab", None, None),
    )
    return jax.shard_map(
        on_device,
        mesh=mesh,
        in_specs=placed,
        out_specs=P("member", "slab", None, None),
        check_vma=False,
    )
```

```python
import functools

import jax
import jax.numpy as jnp
from jax import lax
from jax.experimental import pallas as pl
from jax.experimental.pallas import tpu as pltpu
from jax.sharding import PartitionSpec as P

MESH = pl.DeviceIdType.MESH
F32 = jnp.float32
BF16 = jnp.bfloat16
HIGHEST = lax.Precision.HIGHEST

PEERS = 64
SLABS = 4
ROWS = 8
K = 512
BLKS = 2
MSG = BLKS * ROWS
CELLS = 2048
PIECES = 2
W = CELLS // PIECES
RIM = 256
POOL = 1024
GROUP = 8
GROUPS = PEERS // GROUP


def nt(a, b, precision=None):
    return lax.dot_general(
        a, b, (((1,), (1,)), ((), ())), precision=precision, preferred_element_type=F32
    )


def mm(a, b):
    return jnp.dot(a, b, precision=HIGHEST, preferred_element_type=F32)


def iota(shape, axis):
    return lax.broadcasted_iota(jnp.int32, shape, axis)


def split3(row, width):
    full = jnp.broadcast_to(row, (16, width))
    high = full.astype(BF16).astype(F32)
    rest = full - high
    mid = rest.astype(BF16).astype(F32)
    low = rest - mid
    r = iota((16, width), 0)
    rows = jnp.where(r == 0, high, jnp.where(r == 1, mid, jnp.where(r == 2, low, 0.0)))
    return rows.astype(BF16)


def gather_rows(inverse):
    n = GROUP * MSG
    out, src = iota((n, n), 0), iota((n, n), 1)
    if inverse:
        out, src = src, out
    wanted = (out % ROWS) * MSG + out // ROWS
    return jnp.where(src == wanted, 1.0, 0.0).astype(BF16)


def exchange(
    state, obs_in, vals_in, idx_in, cnt_in, loc_in, out,
    obs, vals, idx, loc, cnt, stage, fsend, frecv, bsend, back, osend, orecv, hsend, hrecv,
    pert, wgt, mats, expand, tbigf, tbig, spert,
    in_sem, st_sem, fs_sem, fr_sem, fl_sem, bs_sem, br_sem,
    os_sem, or_sem, ol_sem, hs_sem, hr_sem, relay,
):
    me = lax.axis_index("member")
    slab = lax.axis_index("slab")
    right = lax.rem(slab + 1, SLABS)
    left = lax.rem(slab + SLABS - 1, SLABS)

    barrier = pltpu.get_barrier_semaphore()

    corner = [
        lax.rem(me // 16 + n // 2, 4) * 16 + lax.rem(me + n, 2) for n in range(8)
    ]

    def plane(dz):
        at = lax.rem(me // 2 + dz, 8) * 2
        return [corner[n] + at for n in range(8)]

    up, down = plane(1)[0], plane(7)[0]

    def signal(semaphore, member):
        pl.semaphore_signal(
            semaphore, inc=1, device_id={"member": member}, device_id_type=MESH
        )

    for d in plane(1) + plane(7) + plane(0)[1:]:
        signal(barrier, d)
    for neighbour in (left, right):
        pl.semaphore_signal(barrier, inc=1, device_id={"slab": neighbour}, device_id_type=MESH)

    fetches = [
        pltpu.make_async_copy(source, target, in_sem.at[n])
        for n, (source, target) in enumerate(
            ((obs_in, obs), (vals_in, vals), (idx_in, idx), (loc_in, loc), (cnt_in, cnt))
        )
    ]
    for fetch in fetches:
        fetch.start()

    def stage_copy(p):
        cols = pl.ds(p * W, W)
        return pltpu.make_async_copy(
            state.at[:, 0, :, cols], stage.at[:, :, cols], st_sem.at[p]
        )

    for p in range(PIECES):
        stage_copy(p).start()
    fetches[0].wait()
    pl.semaphore_wait(barrier, 8 + 8 + 7 + 2)

    def message(r):
        a = obs[:, pl.ds(pl.multiple_of(r * 2 * RIM, 2 * RIM), RIM)].astype(F32)
        b = obs[:, pl.ds(pl.multiple_of(r * 2 * RIM + RIM, RIM), RIM)].astype(F32)
        osend[r] = jnp.concatenate([a, b], axis=0).astype(BF16)

    def send_obs(d):
        message(d)
        pltpu.make_async_remote_copy(
            src_ref=osend.at[d], dst_ref=orecv.at[me], send_sem=os_sem, recv_sem=or_sem,
            device_id={"member": d}, device_id_type=MESH,
        ).start()

    for far in range(1, 5):
        if far in (2, 3):
            pl.semaphore_wait(relay.at[far - 2, 0], 1)
        if far > 1:
            pl.semaphore_wait(relay.at[far - 2, 1], 1)
        if far < 4:
            signal(relay.at[far - 1, 1], up)
        if far < 3:
            signal(relay.at[far - 1, 0], down)
        reach = {1: plane(1) + plane(7), 4: plane(4)}.get(far, plane(far) + plane(8 - far))
        for d in reach + (plane(0)[1:] if far == 1 else []):
            send_obs(d)
    message(me)
    own_obs = pltpu.make_async_copy(osend.at[me], orecv.at[me], ol_sem)
    own_obs.start()
    for fetch in fetches[1:]:
        fetch.wait()

    def forward(p):
        stage_copy(p).wait()
        cols = pl.ds(p * W, W)

        def group(i, carry):
            g = lax.rem(me // GROUP + i, GROUPS)
            first = pl.multiple_of(g * GROUP, GROUP)
            rows = stage[:, pl.ds(pl.multiple_of(g * MSG, MSG), MSG), cols]
            moved = jnp.dot(
                gather_rows(False), rows.reshape(GROUP * MSG, W), preferred_element_type=F32
            )
            fsend[p, pl.ds(first, GROUP)] = moved.astype(BF16).reshape(GROUP, MSG, W)

            def one(j, inner):
                d = first + j

                @pl.when(d != me)
                def _():
                    pltpu.make_async_remote_copy(
                        src_ref=fsend.at[p, d], dst_ref=frecv.at[p, me],
                        send_sem=fs_sem.at[p], recv_sem=fr_sem.at[p],
                        device_id={"member": d}, device_id_type=MESH,
                    ).start()

                return inner

            lax.fori_loop(0, GROUP, one, 0)
            return carry

        lax.fori_loop(0, GROUPS, group, 0)
        pltpu.make_async_copy(fsend.at[p, me], frecv.at[p, me], fl_sem.at[p]).start()

    forward(0)

    own_obs.wait()
    most = pl.ds(0, PEERS - 1)
    pltpu.make_async_copy(osend.at[most], orecv.at[most], or_sem).wait()

    def halves(i, carry):
        x = orecv[pl.ds(i * 8, 8)].astype(F32)
        rows = pl.ds(pl.multiple_of(i * 64, 64), 64)
        hsend[1, rows] = x[:, :ROWS].reshape(64, RIM).astype(BF16)
        hsend[0, rows] = x[:, ROWS:].reshape(64, RIM).astype(BF16)
        return carry

    lax.fori_loop(0, 8, halves, 0)
    v = vals[...].astype(F32)
    for side, at in ((1, 0), (0, RIM)):
        r = iota((16, RIM), 0)
        first, second = v[0:1, at : at + RIM], v[1:2, at : at + RIM]
        hsend[side, K : K + 16] = jnp.where(
            r == 0, first, jnp.where(r == 1, second, 0.0)
        ).astype(BF16)
    halos = [
        pltpu.make_async_remote_copy(
            src_ref=hsend.at[side], dst_ref=hrecv.at[side],
            send_sem=hs_sem.at[side], recv_sem=hr_sem.at[side],
            device_id={"slab": to}, device_id_type=MESH,
        )
        for side, to in ((0, right), (1, left))
    ]
    for halo in halos:
        halo.start()

    for p in range(1, PIECES):
        forward(p)

    def fill_expand(i, carry):
        j = iota((64, POOL), 0) + i * 64
        c = iota((64, POOL), 1)
        rows = pl.ds(pl.multiple_of(i * 64, 64), 64)
        for b in range(BLKS):
            at = (j // ROWS) * MSG + b * ROWS + j % ROWS
            expand[b, rows] = jnp.where(c == at, 1.0, 0.0).astype(BF16)
        return carry

    lax.fori_loop(0, K // 64, fill_expand, 0)

    for halo in halos:
        halo.wait()

    departs, inverses = [], []
    for q, ref in enumerate((hrecv.at[0], hsend.at[1], hsend.at[0], hrecv.at[1])):
        x = ref[:K].astype(F32)
        mean = jnp.sum(x, axis=0, keepdims=True) * (1.0 / K)
        pert[:, q * RIM : (q + 1) * RIM] = (x - mean).astype(BF16)
        tail = ref[K : K + 16].astype(F32)
        departs.append(tail[0:1] - mean)
        inverses.append(tail[1:2])
    depart = split3(jnp.concatenate(departs, axis=1), POOL)

    diagonal = iota((K, K), 0) == iota((K, K), 1)
    for b in range(BLKS):
        row = idx[b : b + 1, :]
        slot = iota((1, 512), 1)
        local = jnp.where(slot < cnt[0, b], loc[b : b + 1, :], 0.0)
        local = split3(local, 512)
        for q in range(4):
            hit = iota((RIM, 512), 0) + q * RIM == row
            hit = jnp.where(hit, 1.0, 0.0).astype(BF16)
            total = nt(local, hit)
            weight = inverses[q] * (total[0:1] + total[1:2] + total[2:3])
            cols = slice(q * RIM, (q + 1) * RIM)
            wgt[b, :, cols] = (pert[:, cols].astype(F32) * weight).astype(BF16)

    def transform(b, carry):
        weighted = wgt[b]
        drive = nt(depart, weighted)
        drive = jnp.broadcast_to(drive[0:1] + drive[1:2] + drive[2:3], (8, K))
        gram = nt(pert[...], weighted) + jnp.where(diagonal, K - 1.0, 0.0)
        scale = jnp.sum(gram * gram, axis=1, keepdims=True)
        scale = jnp.sqrt(jnp.sum(scale, axis=0, keepdims=True))
        matrix = gram * (1.0 / scale)
        factor = jnp.where(diagonal, 1.5, 0.0) - 0.5 * matrix
        mats[1] = factor
        mats[0] = mm(matrix, factor)
        mats[2] = jnp.where(diagonal, 1.5, 0.0) - 0.5 * mm(mats[1], mats[0])
        mats[0] = mm(mats[0], mats[2])
        mats[1] = mm(mats[2], mats[1])
        mats[2] = jnp.where(diagonal, 1.5, 0.0) - 0.5 * mm(mats[1], mats[0])
        mats[0] = mm(mats[2], mats[1])
        inverse = mats[0]
        inner = nt(drive, inverse, HIGHEST)
        shift = nt(inner, inverse, HIGHEST)[0:1] / scale
        spread = jnp.sqrt((K - 1.0) / scale)
        mats[1] = spread * inverse.T + shift

        def widen(i, inner_carry):
            rows = mats[1, pl.ds(pl.multiple_of(i * 128, 128), 128)].astype(BF16)
            wide = jnp.dot(rows, expand[b], preferred_element_type=F32)
            at = pl.ds(pl.multiple_of(b * ROWS, ROWS), ROWS)
            tbigf[pl.ds(i * 16, 16), at] = wide.reshape(16, ROWS, POOL)
            return inner_carry

        lax.fori_loop(0, 4, widen, 0)
        return carry

    lax.fori_loop(0, BLKS, transform, 0)

    def narrow(i, carry):
        rows = pl.ds(pl.multiple_of(i * 128, 128), 128)
        tbig[rows] = tbigf[pl.ds(i * 8, 8)].reshape(128, POOL).astype(BF16)
        return carry

    lax.fori_loop(0, 8, narrow, 0)

    for p in range(PIECES):
        pltpu.make_async_copy(fsend.at[p, me], frecv.at[p, me], fl_sem.at[p]).wait()
        pltpu.make_async_copy(fsend.at[p, most], frecv.at[p, most], fr_sem.at[p]).wait()

        def add_up(i, total):
            x = frecv[p, pl.ds(i * 4, 4)].astype(F32)
            return total + jnp.sum(x, axis=0)

        total = lax.fori_loop(0, 16, add_up, jnp.zeros((MSG, W), F32))
        means = [
            jnp.sum(total[b * ROWS : (b + 1) * ROWS], axis=0, keepdims=True) * (1.0 / K)
            for b in range(BLKS)
        ]
        mean = jnp.concatenate([jnp.broadcast_to(m, (ROWS, W)) for m in means], axis=0)

        def less_mean(i, carry):
            x = frecv[p, pl.ds(i * 4, 4)].astype(F32) - mean[None]
            spert[pl.ds(pl.multiple_of(i * 64, 64), 64)] = x.reshape(64, W).astype(BF16)
            return carry

        lax.fori_loop(0, 16, less_mean, 0)

        def apply(i, carry):
            part = lax.rem(me // 16 + 1 + i, 4)
            rows = tbig[pl.ds(pl.multiple_of(part * 256, 256), 256)]
            moved = jnp.dot(rows, spert[...], preferred_element_type=F32)
            new = moved.reshape(16, MSG, W) + mean[None]
            first = pl.multiple_of(part * 16, 16)
            bsend[p, pl.ds(first, 16)] = new.astype(BF16)

            def one(j, inner):
                step = j // 2
                dz = lax.rem(4 + (1 - 2 * lax.rem(step, 2)) * ((step + 1) // 2) + 8, 8)
                d = first + lax.rem(me // 2 + dz, 8) * 2 + lax.rem(j + me, 2)

                @pl.when(d != me)
                def _():
                    pltpu.make_async_remote_copy(
                        src_ref=bsend.at[p, d], dst_ref=back.at[p, me],
                        send_sem=bs_sem.at[p], recv_sem=br_sem.at[p, me // GROUP],
                        device_id={"member": d}, device_id_type=MESH,
                    ).start()

                return inner

            lax.fori_loop(0, 16, one, 0)
            return carry

        lax.fori_loop(0, 4, apply, 0)
        pltpu.make_async_copy(bsend.at[p, me], back.at[p, me], br_sem.at[p, me // GROUP]).start()

    for p in range(PIECES):

        def place(i, carry):
            y = lax.rem(me // 16 + 3 - i // 2, 4)
            g = y * 2 + lax.rem(i, 2)
            some = pl.ds(pl.multiple_of(g * GROUP, GROUP), GROUP)
            pltpu.make_async_copy(bsend.at[p, some], back.at[p, some], br_sem.at[p, g]).wait()
            moved = jnp.dot(
                gather_rows(True), back[p, some].reshape(GROUP * MSG, W), preferred_element_type=F32
            )
            rows = pl.ds(pl.multiple_of(g * MSG, MSG), MSG)
            out[:, 0, rows, p * W : (p + 1) * W] = moved.astype(BF16).reshape(ROWS, MSG, W)
            return carry

        lax.fori_loop(0, GROUPS, place, 0)

    pltpu.make_async_copy(osend.at[most], orecv.at[most], os_sem).wait()
    for p in range(PIECES):
        pltpu.make_async_copy(fsend.at[p, most], frecv.at[p, most], fs_sem.at[p]).wait()
        pltpu.make_async_copy(bsend.at[p, most], back.at[p, most], bs_sem.at[p]).wait()


def on_device(ensemble_obs, obs_values, obs_index, obs_count, loc_weight, state):
    any_space = pl.BlockSpec(memory_space=pl.ANY)
    vmem = pltpu.VMEM
    dma = pltpu.SemaphoreType.DMA

    def in_hbm(array):
        return pltpu.with_memory_space_constraint(array, pltpu.HBM)

    return pl.pallas_call(
        exchange,
        name="exchange",
        out_shape=vmem(state.shape, BF16),
        in_specs=[any_space] * 6,
        out_specs=pl.BlockSpec(memory_space=vmem),
        scratch_shapes=[
            vmem((ROWS, PEERS * 2 * RIM), BF16),
            vmem((2, 2 * RIM), BF16),
            vmem((BLKS, 512), jnp.int32),
            vmem((BLKS, 512), F32),
            pltpu.SMEM((1, BLKS), jnp.int32),
            vmem((ROWS, PEERS * BLKS, CELLS), BF16),
            vmem((PIECES, PEERS, MSG, W), BF16),
            vmem((PIECES, PEERS, MSG, W), BF16),
            vmem((PIECES, PEERS, MSG, W), BF16),
            vmem((PIECES, PEERS, MSG, W), BF16),
            vmem((PEERS, MSG, RIM), BF16),
            vmem((PEERS, MSG, RIM), BF16),
            vmem((2, K + 16, RIM), BF16),
            vmem((2, K + 16, RIM), BF16),
            vmem((K, POOL), BF16),
            vmem((BLKS, K, POOL), BF16),
            vmem((3, K, K), F32),
            vmem((BLKS, K, POOL), BF16),
            vmem((PEERS, MSG, POOL), F32),
            vmem((BLKS * K, BLKS * K), BF16),
            vmem((BLKS * K, W), BF16),
            dma((5,)), dma((PIECES,)), dma((PIECES,)), dma((PIECES,)), dma((PIECES,)),
            dma((PIECES,)), dma((PIECES, GROUPS)),
            dma, dma, dma, dma((2,)), dma((2,)), pltpu.SemaphoreType.REGULAR((3, 2)),
        ],
        compiler_params=pltpu.CompilerParams(
            collective_id=0, has_side_effects=True, vmem_limit_bytes=48 << 20
        ),
    )(
        in_hbm(state),
        in_hbm(ensemble_obs.reshape(ROWS, PEERS * 2 * RIM)),
        in_hbm(obs_values.reshape(2, 2 * RIM)),
        in_hbm(obs_index.reshape(BLKS, 512)),
        in_hbm(obs_count),
        in_hbm(loc_weight.reshape(BLKS, 512)),
    )


def solution(mesh):
    placed = (
        P("member", "slab", None),
        P(None, "slab", "member"),
        P("slab", "member", None),
        P("slab", "member"),
        P("slab", "member", None),
        P("member", "slab", None, None),
    )
    return jax.shard_map(
        on_device,
        mesh=mesh,
        in_specs=placed,
        out_specs=P("member", "slab", None, None),
        check_vma=False,
    )
```
